256 devices in a mesh: tm: 16 (over y, x), pair: 16 (over z, core).
Axes of the slice: x: 4, y: 4, z: 8, core: 2. Of those that a mesh axis runs over, the one named last changes fastest.
Arguments:
- record: bfloat16 [8192, 16, 256], P('tm', None, 'pair'), may hold values from -6 to 6
- partners: int32 [4096, 64], P(('tm', 'pair')), may hold values from 0 to 4095, as said below
- offsets: int32 [15], replicated, may hold values from 0 to 7168, as said below
Outputs:
- correlations: float32 [4096, 64, 512], P(('tm', 'pair'))
The draws below stay inside these ranges and needn't reach their ends.
Inputs may be any that keep to these rules, and one draw needn't show every extreme that they name: `partners`: row k lists 64 different channels, none equal to k, all with the same value of channel // 256 as k, and each within 400 channels of k. offsets[0] is 0, offsets[14] is 7168, and offsets[s] lies within 128 of s * 512.
All inputs are finite; a program needn't handle non-finite values.
Results may differ from the reference program's by a relative error of at most 0.0051.
Values may be sent and summed in bfloat16 or wider, within the bound.
No kernel may reach another device: no remote copies, remote signals or barrier semaphores. Data moves between devices by JAX's collectives and lax.ppermute only.
A program may use at most 128 MiB of HBM per device.

```python
import math
import jax
import jax.numpy as jnp
from jax import lax

SEG = 1024
NF = 512
NLAG = 512
NPART = 64
OFFSET = 400
TSAMP = 8192
SEGS = 15
SECT = 256
CHANNELS = 4096
N_TM = 16


def draw_partners(key, part):
    span_count = 2 * OFFSET + 1
    channel_ids = jnp.arange(CHANNELS, dtype=jnp.int32)
    local_pos = channel_ids % SECT
    step_range = jnp.arange(span_count, dtype=jnp.int32) - OFFSET
    candidate = local_pos[:, None] + step_range[None, :]
    valid_mask = (candidate >= 0) & (candidate < SECT) & (step_range[None, :] != 0)
    noise_bits = jax.random.randint(key, (CHANNELS, span_count), 0, 1 << 18, dtype=jnp.int32)
    ranked = jnp.where(valid_mask, noise_bits * span_count + step_range[None, :] + OFFSET, -1 - step_range[None, :] - OFFSET)
    top_scores, chosen_idx = lax.top_k(ranked, NPART)
    return channel_ids[:, None] + chosen_idx.astype(jnp.int32) - OFFSET


def draw_offsets(key, part):
    segment_ids = jnp.arange(SEGS, dtype=jnp.int32)
    centers = segment_ids * (SEG // 2)
    jitter = jax.random.randint(key, (SEGS,), -(SEG // 8), SEG // 8 + 1, dtype=jnp.int32)
    inner_mask = (segment_ids > 0) & (segment_ids < SEGS - 1)
    return centers + jnp.where(inner_mask, jitter, 0)


def level_of(stream_key, extent, split, smallest, top_value):
    loudness = 1.0
    for dim, blocks in split:
        heights = jax.random.uniform(jax.random.fold_in(jax.random.fold_in(stream_key, 6), dim), (blocks,), jnp.float32, smallest / len(split), top_value / len(split))
        loudness = loudness * jnp.repeat(jnp.exp(heights), extent[dim] // blocks).reshape((-1,) + (1,) * (len(extent) - 1 - dim))
    return loudness


def noise(own_key, shape, scale, reach, shards=(), kind=jnp.bfloat16):
    values = jax.random.normal(own_key, shape, jnp.float32) * scale
    if len(shards) > 0:
        values = level_of(own_key, shape, shards, -0.22, 0.18) * values
    return jnp.clip(values, min=-reach, max=reach).astype(kind)


def setup_inputs(seed: int = 0) -> dict:
    keys = jax.random.split(jax.random.key(seed), 4)
    record = noise(keys[0], (TSAMP, N_TM, SECT), 1.0, 6.0, ((0, 16), (2, 16)))
    partners = draw_partners(jax.random.fold_in(keys[3], 71), 0)
    offsets = draw_offsets(jax.random.fold_in(keys[3], 71), 0)
    return dict(record=record, partners=partners, offsets=offsets)


def build_tables(band_count):
    band_width = NF // band_count
    column = jnp.arange(2 * NF, dtype=jnp.int32)
    inside = column % (2 * band_width)
    imag_part = inside >= band_width
    frequency = column // (2 * band_width) * band_width + inside % band_width
    samples = jnp.arange(SEG, dtype=jnp.int32)
    sample_phase = jnp.remainder(samples[:, None] * frequency[None, :], SEG).astype(jnp.float32) * (2.0 * math.pi / SEG)
    hann_taper = 0.5 - 0.5 * jnp.cos(samples.astype(jnp.float32) * (2.0 * math.pi / SEG))
    forward = (hann_taper[:, None] * jnp.where(imag_part[None, :], -jnp.sin(sample_phase), jnp.cos(sample_phase))).astype(jnp.bfloat16)
    lag_index = jnp.arange(NLAG, dtype=jnp.int32) - NLAG // 2
    lag_phase = jnp.remainder(frequency[:, None] * lag_index[None, :], SEG).astype(jnp.float32) * (2.0 * math.pi / SEG)
    inverse = jnp.where(imag_part[:, None], -jnp.sin(lag_phase), jnp.cos(lag_phase)).astype(jnp.bfloat16)
    return (forward, inverse)

def segment_rows(series, offsets):
    return jax.vmap(lambda start: lax.dynamic_slice_in_dim(series, start, SEG, 0))(offsets)

def whiten(spectrum, band_count):
    band_width = spectrum.shape[-1] // (2 * band_count)
    shaped = spectrum.reshape(spectrum.shape[:-1] + (band_count, 2, band_width))
    power_sum = lax.optimization_barrier(jnp.sum(shaped * shaped, axis=-2, keepdims=True))
    water_level = lax.optimization_barrier(jnp.mean(power_sum, axis=(-3, -1), keepdims=True)) + 1e-06
    scaled = shaped * lax.rsqrt(power_sum + water_level)
    return scaled.reshape(spectrum.shape).astype(jnp.bfloat16)

def cross_spectrum(own_rows, chosen, band_count):
    band_width = own_rows.shape[-1] // (2 * band_count)
    own_parts = own_rows.astype(jnp.float32).reshape(own_rows.shape[0], 1, own_rows.shape[1], band_count, 2, band_width)
    chosen_parts = chosen.astype(jnp.float32).reshape(chosen.shape[:3] + (band_count, 2, band_width))
    real_sum = lax.optimization_barrier(jnp.sum(own_parts[..., 0, :] * chosen_parts[..., 0, :] + own_parts[..., 1, :] * chosen_parts[..., 1, :], axis=2))
    imag_sum = lax.optimization_barrier(jnp.sum(own_parts[..., 0, :] * chosen_parts[..., 1, :] - own_parts[..., 1, :] * chosen_parts[..., 0, :], axis=2))
    stacked = jnp.stack([real_sum, imag_sum], axis=-2)
    return stacked.reshape(chosen.shape[0], chosen.shape[1], own_rows.shape[-1]).astype(jnp.bfloat16)

def correlate(own_rows, window, group_picks, inverse, band_count):
    chosen = window[group_picks]
    crossed = cross_spectrum(own_rows, chosen, band_count)
    lag_values = jnp.dot(crossed.reshape(-1, crossed.shape[-1]), inverse, preferred_element_type=jnp.float32)
    return lag_values.reshape(crossed.shape[0], crossed.shape[1], inverse.shape[1]) * (1.0 / math.sqrt(NF))

def reference(record, partners, offsets):
    forward, inverse = build_tables(1)
    section = record.shape[2]
    section_count = record.shape[1]
    partner_count = partners.shape[1]
    by_section = jnp.moveaxis(record, 1, 0)
    section_picks = partners.reshape(section_count, section, partner_count) % section

    def one_section(section_args):
        series, row_picks = section_args
        pieces = segment_rows(series, offsets)
        spectrum = jnp.einsum('stn,tf->nsf', pieces.astype(jnp.float32), forward.astype(jnp.float32))
        whitened = whiten(spectrum, 1)

        def one_group(group_args):
            own_rows, group_picks = group_args
            return correlate(own_rows, whitened, group_picks, inverse, 1)
        grouped = lax.map(one_group, (whitened.reshape(section // 8, 8, whitened.shape[1], whitened.shape[2]), row_picks.reshape(section // 8, 8, partner_count)))
        return grouped.reshape(section, partner_count, inverse.shape[1])
    result = lax.map(one_section, (by_section, section_picks))
    return result.reshape(section_count * section, partner_count, inverse.shape[1])
```

```python
import functools
import math

import jax
import jax.numpy as jnp
import numpy as np
from jax import lax
from jax.experimental import pallas as pl
from jax.experimental.pallas import tpu as pltpu
from jax.sharding import PartitionSpec as P

SEG = 1024
NF = 512
NLAG = 512
SEGS = 15
SLOTS = 16
NPART = 64
TSAMP = 8192
SHARDS = 16
SHARD = TSAMP // SHARDS
SECT = 256
OWN = 16
FB = 8
BLOCKS = NF // FB
F32 = jnp.float32
BF16 = jnp.bfloat16
NT = (((1,), (1,)), ((), ()))
NN = (((1,), (0,)), ((), ()))


def build_tables():
    column = np.arange(2 * NF)
    imag_part = column >= NF
    frequency = column % NF
    samples = np.arange(SEG)
    phase = (samples[:, None] * frequency[None, :] % SEG).astype(np.float32) * np.float32(2.0 * math.pi / SEG)
    taper = 0.5 - 0.5 * np.cos(samples.astype(np.float32) * np.float32(2.0 * math.pi / SEG))
    forward = taper[:, None] * np.where(imag_part[None, :], -np.sin(phase), np.cos(phase))
    lag = np.arange(NLAG) - NLAG // 2
    lag_phase = (frequency[:, None] * lag[None, :] % SEG).astype(np.float32) * np.float32(2.0 * math.pi / SEG)
    inverse = np.where(imag_part[:, None], -np.sin(lag_phase), np.cos(lag_phase))
    return np.ascontiguousarray(forward.T.astype(jnp.bfloat16)), inverse.astype(jnp.bfloat16)


def dot(a, b, dims):
    return lax.dot_general(a, b, dims, preferred_element_type=F32)


def kernel(offsets, series_hbm, forward, inverse, spread, picks, out_hbm,
           series, piece, spectrum, white, grams, chosen, result, in_sem, out_sem):
    copies = [
        pltpu.make_async_copy(series_hbm.at[:, t], series.at[:, :, pl.ds(t * SHARD, SHARD)], in_sem.at[t])
        for t in range(SHARDS)
    ]
    for c in copies:
        c.start()
    white[:, :, SEGS] = jnp.zeros((BLOCKS, 2, FB, SECT), F32)
    lane = lax.broadcasted_iota(jnp.int32, (SECT, 128), 1)
    for c in copies:
        c.wait()

    def segment(s, carry):
        start = offsets[s]
        base = start // 128
        off = start % 128
        back = (128 - off) % 128
        keep = lane < 128 - off

        def tile(i):
            at = pl.multiple_of(jnp.minimum(base + i, TSAMP // 128 - 1) * 128, 128)
            rows = series[:, :, pl.ds(at, 128)].reshape(SECT, 128)
            return pltpu.roll(rows.astype(F32), back, 1)

        here = tile(0)
        for i in range(SEG // 128):
            after = tile(i + 1)
            piece[:, i * 128:(i + 1) * 128] = jnp.where(keep, here, after).astype(BF16)
            here = after
        spectrum[...] = dot(forward[...], piece[...], NT)
        total = jnp.zeros((FB, SECT), F32)
        for b in range(BLOCKS):
            re = spectrum[b * FB:(b + 1) * FB, :]
            im = spectrum[NF + b * FB:NF + (b + 1) * FB, :]
            total += re * re + im * im
        water = jnp.sum(total, axis=0, keepdims=True) * (1.0 / NF) + 1e-06
        for b in range(BLOCKS):
            re = spectrum[b * FB:(b + 1) * FB, :]
            im = spectrum[NF + b * FB:NF + (b + 1) * FB, :]
            factor = lax.rsqrt(re * re + im * im + water)
            white[b, 0, s] = re * factor
            white[b, 1, s] = im * factor
        return carry

    lax.fori_loop(0, SEGS, segment, 0)

    half = SLOTS * FB
    mask = (
        lax.broadcasted_iota(jnp.int32, (OWN * FB, 2 * half), 0) % FB
        == lax.broadcasted_iota(jnp.int32, (OWN * FB, 2 * half), 1) % FB
    )
    zero = jnp.zeros((OWN * FB, 2 * half), F32)

    def gram(b):
        rows = white[b].reshape(2 * half, SECT).astype(BF16)
        own = dot(spread[...], rows, NT)
        own = jnp.where(mask, own, zero)
        turned = jnp.concatenate([-own[:, half:], own[:, :half]], axis=1)
        both = jnp.concatenate([own, turned], axis=0).astype(BF16)
        return dot(both, rows, NN).reshape(2, OWN, FB, SECT)

    def pair_of_blocks(b, carry):
        low, high = gram(2 * b), gram(2 * b + 1)
        for k in range(OWN):
            for ri in range(2):
                grams[k, ri, b] = jnp.concatenate([low[ri, k], high[ri, k]], axis=0).astype(BF16)
        return carry

    lax.fori_loop(0, BLOCKS // 2, pair_of_blocks, 0)

    GROUP = 4
    outs = [
        pltpu.make_async_copy(
            result.at[pl.ds(g * GROUP, GROUP)], out_hbm.at[pl.ds(g * GROUP, GROUP)], out_sem.at[g]
        )
        for g in range(OWN // GROUP)
    ]
    for g in range(OWN // GROUP):
        for k in range(g * GROUP, (g + 1) * GROUP):
            crossed = dot(picks[k], grams[k].reshape(2 * NF, SECT), NT)
            chosen[k % GROUP] = crossed.astype(BF16)
        lags = dot(chosen[...].reshape(GROUP * NPART, 2 * NF), inverse[...], NN) * (1.0 / math.sqrt(NF))
        result[g * GROUP:(g + 1) * GROUP] = lags.reshape(GROUP, NPART, NLAG)
        outs[g].start()
    for o in outs:
        o.wait()


def per_device(record, partners, offsets):
    forward, inverse = (jnp.asarray(t) for t in build_tables())
    by_section = jnp.transpose(record, (1, 2, 0))
    mine = lax.all_to_all(by_section, "tm", split_axis=0, concat_axis=0, tiled=True)
    series = lax.all_gather(mine, "pair", axis=0)
    place = lax.axis_index("pair")
    channel = lax.broadcasted_iota(jnp.int32, (OWN * FB, SECT), 1)
    own = place * OWN + lax.broadcasted_iota(jnp.int32, (OWN * FB, SECT), 0) // FB
    spread = (channel == own).astype(BF16)
    picks = ((partners % SECT)[:, :, None] == jnp.arange(SECT, dtype=jnp.int32)).astype(BF16)
    vmem = pl.BlockSpec(memory_space=pltpu.VMEM)
    any_ = pl.BlockSpec(memory_space=pl.ANY)
    return pl.pallas_call(
        kernel,
        out_shape=jax.ShapeDtypeStruct((OWN, NPART, NLAG), F32),
        in_specs=[pl.BlockSpec(memory_space=pltpu.SMEM), any_, vmem, vmem, vmem, vmem],
        out_specs=any_,
        scratch_shapes=[
            pltpu.VMEM((SECT // OWN, OWN, TSAMP), BF16),
            pltpu.VMEM((SECT, SEG), BF16),
            pltpu.VMEM((2 * NF, SECT), F32),
            pltpu.VMEM((BLOCKS, 2, SLOTS, FB, SECT), F32),
            pltpu.VMEM((OWN, 2, BLOCKS // 2, 2 * FB, SECT), BF16),
            pltpu.VMEM((4, NPART, 2 * NF), BF16),
            pltpu.VMEM((OWN, NPART, NLAG), F32),
            pltpu.SemaphoreType.DMA((SHARDS,)),
            pltpu.SemaphoreType.DMA((OWN // 4,)),
        ],
        compiler_params=pltpu.CompilerParams(vmem_limit_bytes=56 * 1024 * 1024),
        name="correlate",
    )(offsets, series, forward, inverse, spread, picks)


def solution(mesh):
    in_specs = (P("tm", None, "pair"), P(("tm", "pair"), None), P())
    out_specs = P(("tm", "pair"), None, None)
    return jax.shard_map(
        per_device, mesh=mesh, in_specs=in_specs, out_specs=out_specs, check_vma=False
    )
```

```python
import functools
import math

import jax
import jax.numpy as jnp
import numpy as np
from jax import lax
from jax.experimental import pallas as pl
from jax.experimental.pallas import tpu as pltpu
from jax.sharding import PartitionSpec as P

SEG = 1024
NF = 512
NLAG = 512
SEGS = 15
PAIRS = 8
NPART = 64
SHARDS = 16
SHARD = 512
SECT = 256
OWN = 16
HALF = 128
FB = 8
BLOCKS = NF // FB
TILES = 16
F32 = jnp.float32
BF16 = jnp.bfloat16
NT = (((1,), (1,)), ((), ()))
NN = (((1,), (0,)), ((), ()))


def slots():
    q = np.arange(128)
    freq = np.concatenate([q, 512 - q, 256 + q, 256 - q])
    freq[128], freq[384] = 128, 384
    sign = np.where(np.arange(512) < 384, 1.0, -1.0)
    return freq, sign


def build_tables():
    samples = np.arange(SEG)
    unit = np.float32(2.0 * math.pi / SEG)
    taper = (0.5 - 0.5 * np.cos(samples.astype(np.float32) * unit)).astype(np.float32)
    q = np.arange(128)
    phase = (q[:, None] * samples[None, :] % SEG).astype(np.float32) * unit
    cosine, sine = taper * np.cos(phase), -taper * np.sin(phase)
    eighth = (128 * samples % SEG).astype(np.float32) * unit
    sine[0] = np.where(samples % 4 == 2, -taper * np.sin(eighth), taper * np.cos(eighth))
    sine[0] = np.where(samples % 4 == 2, -1.0, np.where(samples % 4 == 3, -1.0, 1.0)) * sine[0]
    forward = np.concatenate([cosine, sine]).reshape(256, 256, 4).transpose(2, 0, 1)
    freq, sign = slots()
    lag = np.arange(NLAG) - NLAG // 2
    lag_phase = (freq[:, None] * lag[None, :] % SEG).astype(np.float32) * unit
    inverse = np.concatenate([np.cos(lag_phase), -sign[:, None] * np.sin(lag_phase)])
    return np.ascontiguousarray(forward).astype(jnp.bfloat16), inverse.astype(jnp.bfloat16)


def dot(a, b, dims):
    return lax.dot_general(a, b, dims, preferred_element_type=F32)


def cut_pieces(offsets, series, piece, u, slot):
    lane = lax.broadcasted_iota(jnp.int32, (HALF, 128), 1)
    for s2 in range(2):
        start = offsets[min(2 * u + s2, SEGS - 1)]
        for r in range(4):
            first = start + r
            group = pl.multiple_of((first & 3) * 128, 128)
            at = first >> 2
            tile, off = at >> 7, at & 127
            back = (128 - off) & 127
            keep = lane < 128 - off
            turned = []
            for i in range(3):
                t = jnp.minimum(tile + i, SHARDS - 1)
                rows = series[:, t, :, pl.ds(group, 128)].reshape(HALF, 128)
                turned.append(pltpu.roll(rows.astype(F32), back, 1))
            for i in range(2):
                piece[slot, r, s2 * HALF:(s2 + 1) * HALF, i * 128:(i + 1) * 128] = jnp.where(
                    keep, turned[i], turned[i + 1]
                ).astype(BF16)


def transform(forward, piece, part, slot):
    for r in range(4):
        part[slot, r] = dot(forward[r], piece[slot, r], NT)


def whiten(part, full, white, u, slot, lanes):
    head = lax.broadcasted_iota(jnp.int32, (FB, SECT), 0) == 0
    total = jnp.zeros((FB, SECT), F32)
    for i in range(TILES):
        c = [part[slot, r, i * FB:(i + 1) * FB, :] for r in range(4)]
        s = [part[slot, r, HALF + i * FB:HALF + (i + 1) * FB, :] for r in range(4)]
        a, b = c[0] + c[2], c[0] - c[2]
        e, g = s[0] + s[2], s[0] - s[2]
        d, k = c[1] - c[3], s[1] - s[3]
        p, h = c[1] + c[3], s[1] + s[3]
        re = [a + p, a - p, b + k, b - k]
        im = [e + h, h - e, g - d, g + d]
        if i == 0:
            im[0] = jnp.where(head, 0.0, im[0])
            re[1] = jnp.where(head, s[0] + k, re[1])
            im[1] = jnp.where(head, -h - s[2], im[1])
            re[2] = jnp.where(head, b, re[2])
            im[2] = jnp.where(head, -d, im[2])
            re[3] = jnp.where(head, s[0] - k, re[3])
            im[3] = jnp.where(head, h - s[2], im[3])
        for j in range(4):
            full[0, j, i], full[1, j, i] = re[j], im[j]
            total += re[j] * re[j] + im[j] * im[j]
    water = jnp.sum(total, axis=0, keepdims=True) * (1.0 / NF) + 1e-06
    for i in range(TILES):
        for j in range(4):
            re, im = full[0, j, i], full[1, j, i]
            factor = lax.rsqrt(re * re + im * im + water)
            for ri, v in ((0, re * factor), (1, im * factor)):
                white[j * TILES + i, ri, u, :, lanes] = jnp.concatenate(
                    [v[:, :HALF], v[:, HALF:]], axis=0
                ).astype(BF16)


def spectra(offsets, series, forward, piece, part, full, white, lanes):
    cut_pieces(offsets, series, piece, 0, 0)
    for u in range(PAIRS):
        transform(forward, piece, part, u % 2)
        if u + 1 < PAIRS:
            cut_pieces(offsets, series, piece, u + 1, (u + 1) % 2)
        whiten(part, full.at[u % 2], white, u, u % 2, lanes)


def near_kernel(offsets, *refs):
    blocks, (forward, white, series, piece, part, full, sem) = refs[:8], refs[8:]
    copies = [pltpu.make_async_copy(b, series.at[i], sem.at[i]) for i, b in enumerate(blocks)]
    for c in copies:
        c.start()
    for c in copies:
        c.wait()
    spectra(offsets, series, forward, piece, part, full, white, slice(0, HALF))


def own_kernel(white, spread, own):
    row = lax.broadcasted_iota(jnp.int32, (HALF, 2 * HALF), 0)
    column = lax.broadcasted_iota(jnp.int32, (HALF, 2 * HALF), 1)
    mask = (row % FB == column % FB) & (column % HALF < SEGS * FB)

    def rows(b, carry):
        spreaded = dot(spread[...], white[b].reshape(2 * HALF, HALF), NT)
        own[b] = jnp.where(mask, spreaded, 0.0).astype(BF16)
        return carry

    lax.fori_loop(0, BLOCKS, rows, 0, unroll=8)


def scratch():
    return [
        pltpu.VMEM((8, SHARDS, OWN, SHARD), BF16),
        pltpu.VMEM((2, 4, SECT, 256), BF16),
        pltpu.VMEM((2, 4, SECT, SECT), F32),
        pltpu.VMEM((2, 2, 4, TILES, FB, SECT), F32),
    ]


VMEM_SPEC = pl.BlockSpec(memory_space=pltpu.VMEM)
ANY_SPEC = pl.BlockSpec(memory_space=pl.ANY)
SMEM_SPEC = pl.BlockSpec(memory_space=pltpu.SMEM)


def near_spectra(offsets, blocks, forward):
    return pl.pallas_call(
        near_kernel,
        out_shape=jax.ShapeDtypeStruct((BLOCKS, 2, PAIRS, 2 * FB, HALF), BF16),
        in_specs=[SMEM_SPEC] + [ANY_SPEC] * 8 + [VMEM_SPEC],
        out_specs=VMEM_SPEC,
        scratch_shapes=scratch() + [pltpu.SemaphoreType.DMA((8,))],
        compiler_params=pltpu.CompilerParams(vmem_limit_bytes=16 * 1024 * 1024),
        cost_estimate=pl.CostEstimate(flops=5_000_000_000, bytes_accessed=7_000_000, transcendentals=0),
        name="near_spectra",
    )(offsets, *blocks, forward)


def own_operand(white):
    spread = (np.arange(HALF)[:, None] // FB == np.arange(HALF)[None, :]).astype(jnp.bfloat16)
    return pl.pallas_call(
        own_kernel,
        out_shape=jax.ShapeDtypeStruct((BLOCKS, HALF, SECT), BF16),
        in_specs=[VMEM_SPEC] * 2,
        out_specs=VMEM_SPEC,
        compiler_params=pltpu.CompilerParams(vmem_limit_bytes=16 * 1024 * 1024),
        cost_estimate=pl.CostEstimate(flops=4_000_000_000, bytes_accessed=9_000_000, transcendentals=0),
        name="own_operand",
    )(white, jnp.asarray(spread))


GROUP = 4


def second_kernel(places, offsets, *refs):
    n = len(places)
    blocks, refs = refs[:n], refs[n:]
    (white_hbm, own_hbm, forward, inverse, picks, out_hbm, series, piece, part, full, white, own,
     grams, chosen, result, sem, near_sem, own_sem, out_sem) = refs
    copies = []
    core = offsets[SEGS]
    for i, (b, (at, part_of)) in enumerate(zip(blocks, places)):
        first, count = ((0, SHARDS), (core * 8, 8), (8 - core * 8, 8))[part_of]
        copies.append(pltpu.make_async_copy(b, series.at[at, pl.ds(first, count)], sem.at[i]))
    for c in copies:
        c.start()
    near = pltpu.make_async_copy(white_hbm, white.at[:, :, :, :, pl.ds(0, HALF)], near_sem)
    near.start()
    mine = pltpu.make_async_copy(own_hbm, own, own_sem)
    mine.start()
    for c in copies:
        c.wait()
    spectra(offsets, series, forward, piece, part, full, white, slice(HALF, SECT))
    near.wait()
    mine.wait()

    def gram(b):
        rows = own[b]
        turned = jnp.concatenate([-rows[:, HALF:], rows[:, :HALF]], axis=1)
        both = jnp.concatenate([rows, turned], axis=0)
        return dot(both, white[b].reshape(2 * HALF, SECT), NN).reshape(2, OWN, FB, SECT)

    def pair_of_blocks(b, carry):
        low, high = gram(2 * b), gram(2 * b + 1)
        for k in range(OWN):
            for ri in range(2):
                grams[k, ri, b] = jnp.concatenate([low[ri, k], high[ri, k]], axis=0).astype(BF16)
        return carry

    lax.fori_loop(0, BLOCKS // 2, pair_of_blocks, 0, unroll=8)
    outs = [
        pltpu.make_async_copy(
            result.at[pl.ds(g * GROUP, GROUP)], out_hbm.at[pl.ds(g * GROUP, GROUP)], out_sem.at[g]
        )
        for g in range(OWN // GROUP)
    ]
    for g in range(OWN // GROUP):
        for k in range(g * GROUP, (g + 1) * GROUP):
            crossed = dot(picks[k], grams[k].reshape(2 * NF, SECT), NT)
            chosen[k % GROUP] = crossed.astype(BF16)
        lags = dot(chosen[...].reshape(GROUP * NPART, 2 * NF), inverse[...], NN) * (1.0 / math.sqrt(NF))
        result[g * GROUP:(g + 1) * GROUP] = lags.reshape(GROUP, NPART, NLAG)
        outs[g].start()
    for o in outs:
        o.wait()


def second_half(offsets, blocks, places, white, own, forward, inverse, picks):
    n = len(blocks)
    return pl.pallas_call(
        functools.partial(second_kernel, places),
        out_shape=jax.ShapeDtypeStruct((OWN, NPART, NLAG), F32),
        in_specs=[SMEM_SPEC] + [ANY_SPEC] * (n + 2) + [VMEM_SPEC] * 3,
        out_specs=ANY_SPEC,
        scratch_shapes=scratch() + [
            pltpu.VMEM((BLOCKS, 2, PAIRS, 2 * FB, SECT), BF16),
            pltpu.VMEM((BLOCKS, HALF, SECT), BF16),
            pltpu.VMEM((OWN, 2, BLOCKS // 2, 2 * FB, SECT), BF16),
            pltpu.VMEM((GROUP, NPART, 2 * NF), BF16),
            pltpu.VMEM((OWN, NPART, NLAG), F32),
            pltpu.SemaphoreType.DMA((n,)),
            pltpu.SemaphoreType.DMA,
            pltpu.SemaphoreType.DMA,
            pltpu.SemaphoreType.DMA((OWN // GROUP,)),
        ],
        compiler_params=pltpu.CompilerParams(vmem_limit_bytes=34 * 1024 * 1024),
        cost_estimate=pl.CostEstimate(flops=8_000_000_000, bytes_accessed=20_000_000, transcendentals=0),
        name="far_and_cross",
    )(offsets, *blocks, white, own, forward, inverse, picks)


def per_device(record, partners, offsets):
    forward, inverse = (jnp.asarray(t) for t in build_tables())
    place = lax.axis_index("pair")
    core = place % 2
    rows = jnp.transpose(record, (1, 2, 0)).reshape(SHARDS * OWN, SHARD)
    order = np.arange(SHARD) % 128 * 4 + np.arange(SHARD) // 128
    sort = (np.arange(SHARD)[:, None] == order[None, :]).astype(jnp.bfloat16)
    rows = jnp.dot(rows, jnp.asarray(sort), preferred_element_type=BF16)
    mine = lax.all_to_all(
        rows.reshape(SHARDS, OWN, SHARD), "tm", split_axis=0, concat_axis=0, tiled=True
    )

    onward = [(i, (i + 2 - 4 * (i % 2)) % 16) for i in range(16)]
    across = [(i, i ^ 1) for i in range(16)]

    def send(v, pairs):
        return lax.ppermute(v, "pair", pairs)

    def half(v):
        return lax.dynamic_slice_in_dim(v, core * 8, 8, 0)

    tie = lax.optimization_barrier
    other = send(mine, across)
    m1, o1 = send(mine, onward), send(other, onward)
    m2, o2 = send(m1, onward), send(o1, onward)
    xm1, xo1 = send(m1, across), send(o1, across)
    m3, o3 = send(m2, onward), send(o2, onward)
    xm2, xo2 = send(m2, across), send(o2, across)
    near = [mine, other, m1, o1, xm1, xo1, m2, o2]
    numbers = jnp.concatenate([offsets, core[None]])
    white = near_spectra(numbers, near, forward)
    m3, o3, white = tie((m3, o3, white))
    m4, o4 = send(half(m3), onward), send(half(o3), onward)
    xm3, xo3 = send(m3, across), send(o3, across)
    own = own_operand(white)
    m4, o4, own = tie((m4, o4, own))
    xm4, xo4 = send(m4, across), send(o4, across)

    far = [xm2, xo2, m3, o3, xm3, xo3, m4, xo4, o4, xm4]
    places = [(i, 0) for i in range(6)] + [(6, 1), (6, 2), (7, 1), (7, 2)]

    toward = 2 * (2 * core - 1)
    steps = np.array([0, 0, 1, 1, -1, -1, 2, 2, -2, -2, 3, 3, -3, -3, 4, 4], np.int32)
    swap = np.array([0, 1, 0, 1, 1, 0, 0, 1, 1, 0, 0, 1, 1, 0, 0, 1], np.int32)
    origin = ((place + toward * steps) % 16) ^ swap
    channel = jnp.repeat(origin * OWN, OWN) + np.tile(np.arange(OWN, dtype=np.int32), 16)
    picks = ((partners % SECT)[:, :, None] == channel).astype(BF16)
    return second_half(numbers, far, places, white, own, forward, inverse, picks)


def solution(mesh):
    in_specs = (P("tm", None, "pair"), P(("tm", "pair"), None), P())
    out_specs = P(("tm", "pair"), None, None)
    return jax.shard_map(
        per_device, mesh=mesh, in_specs=in_specs, out_specs=out_specs, check_vma=False
    )
```

```python
import functools
import math

import jax
import jax.numpy as jnp
import numpy as np
from jax import lax
from jax.experimental import pallas as pl
from jax.experimental.pallas import tpu as pltpu
from jax.sharding import PartitionSpec as P

SEG = 1024
NF = 512
NLAG = 512
SEGS = 15
PAIRS = 8
NPART = 64
SHARDS = 16
SHARD = 512
SECT = 256
OWN = 16
HALF = 128
FB = 8
BLOCKS = NF // FB
TILES = 16
F32 = jnp.float32
BF16 = jnp.bfloat16
NT = (((1,), (1,)), ((), ()))
NN = (((1,), (0,)), ((), ()))


def slots():
    q = np.arange(128)
    freq = np.concatenate([q, 512 - q, 256 + q, 256 - q])
    freq[128], freq[384] = 128, 384
    sign = np.where(np.arange(512) < 384, 1.0, -1.0)
    return freq, sign


def build_tables():
    samples = np.arange(SEG)
    unit = np.float32(2.0 * math.pi / SEG)
    taper = (0.5 - 0.5 * np.cos(samples.astype(np.float32) * unit)).astype(np.float32)
    q = np.arange(128)
    phase = (q[:, None] * samples[None, :] % SEG).astype(np.float32) * unit
    cosine, sine = taper * np.cos(phase), -taper * np.sin(phase)
    eighth = (128 * samples % SEG).astype(np.float32) * unit
    sine[0] = np.where(samples % 4 == 2, -taper * np.sin(eighth), taper * np.cos(eighth))
    sine[0] = np.where(samples % 4 == 2, -1.0, np.where(samples % 4 == 3, -1.0, 1.0)) * sine[0]
    forward = np.concatenate([cosine, sine]).reshape(256, 256, 4).transpose(2, 0, 1)
    freq, sign = slots()
    lag = np.arange(NLAG) - NLAG // 2
    lag_phase = (freq[:, None] * lag[None, :] % SEG).astype(np.float32) * unit
    inverse = np.concatenate([np.cos(lag_phase), -sign[:, None] * np.sin(lag_phase)])
    return np.ascontiguousarray(forward).astype(jnp.bfloat16), inverse.astype(jnp.bfloat16)


def dot(a, b, dims):
    return lax.dot_general(a, b, dims, preferred_element_type=F32)


def cut_pieces(offsets, series, piece, u, slot):
    lane = lax.broadcasted_iota(jnp.int32, (HALF, 128), 1)
    for s2 in range(2):
        start = offsets[min(2 * u + s2, SEGS - 1)]
        for r in range(4):
            first = start + r
            group = pl.multiple_of((first & 3) * 128, 128)
            at = first >> 2
            tile, off = at >> 7, at & 127
            back = (128 - off) & 127
            keep = lane < 128 - off
            turned = []
            for i in range(3):
                t = jnp.minimum(tile + i, SHARDS - 1)
                rows = series[:, t, :, pl.ds(group, 128)].reshape(HALF, 128)
                turned.append(pltpu.roll(rows.astype(F32), back, 1))
            for i in range(2):
                piece[slot, r, s2 * HALF:(s2 + 1) * HALF, i * 128:(i + 1) * 128] = jnp.where(
                    keep, turned[i], turned[i + 1]
                ).astype(BF16)


def transform(forward, piece, part, slot):
    for r in range(4):
        part[slot, r] = dot(forward[r], piece[slot, r], NT)


def whiten(part, full, white, u, slot, lanes):
    head = lax.broadcasted_iota(jnp.int32, (FB, SECT), 0) == 0
    total = jnp.zeros((FB, SECT), F32)
    for i in range(TILES):
        c = [part[slot, r, i * FB:(i + 1) * FB, :] for r in range(4)]
        s = [part[slot, r, HALF + i * FB:HALF + (i + 1) * FB, :] for r in range(4)]
        a, b = c[0] + c[2], c[0] - c[2]
        e, g = s[0] + s[2], s[0] - s[2]
        d, k = c[1] - c[3], s[1] - s[3]
        p, h = c[1] + c[3], s[1] + s[3]
        re = [a + p, a - p, b + k, b - k]
        im = [e + h, h - e, g - d, g + d]
        if i == 0:
            im[0] = jnp.where(head, 0.0, im[0])
            re[1] = jnp.where(head, s[0] + k, re[1])
            im[1] = jnp.where(head, -h - s[2], im[1])
            re[2] = jnp.where(head, b, re[2])
            im[2] = jnp.where(head, -d, im[2])
            re[3] = jnp.where(head, s[0] - k, re[3])
            im[3] = jnp.where(head, h - s[2], im[3])
        for j in range(4):
            full[0, j, i], full[1, j, i] = re[j], im[j]
            total += re[j] * re[j] + im[j] * im[j]
    water = jnp.sum(total, axis=0, keepdims=True) * (1.0 / NF) + 1e-06
    for i in range(TILES):
        for j in range(4):
            re, im = full[0, j, i], full[1, j, i]
            factor = lax.rsqrt(re * re + im * im + water)
            for ri, v in ((0, re * factor), (1, im * factor)):
                white[j * TILES + i, ri, u, :, lanes] = jnp.concatenate(
                    [v[:, :HALF], v[:, HALF:]], axis=0
                ).astype(BF16)


def spectra(offsets, series, forward, piece, part, full, white, lanes, after=lambda u: None):
    cut_pieces(offsets, series, piece, 0, 0)
    for u in range(PAIRS):
        transform(forward, piece, part, u % 2)
        if u + 1 < PAIRS:
            cut_pieces(offsets, series, piece, u + 1, (u + 1) % 2)
        whiten(part, full.at[u % 2], white, u, u % 2, lanes)
        after(u)


def near_kernel(offsets, *refs):
    blocks, refs = refs[:8], refs[8:]
    (forward, spread, white_hbm, own_hbm, token, white, own, series, piece, part, full, sem, near_sem,
     own_sem) = refs
    copies = [pltpu.make_async_copy(b, series.at[i], sem.at[i]) for i, b in enumerate(blocks)]
    for c in copies:
        c.start()
    for c in copies:
        c.wait()
    kept = [
        pltpu.make_async_copy(white.at[:, :, u], white_hbm.at[:, :, u], near_sem.at[u])
        for u in range(PAIRS)
    ]
    spectra(
        offsets, series, forward, piece, part, full, white, slice(0, HALF), lambda u: kept[u].start()
    )
    token[...] = jnp.zeros((8, 128), F32)
    row = lax.broadcasted_iota(jnp.int32, (HALF, 2 * HALF), 0)
    column = lax.broadcasted_iota(jnp.int32, (HALF, 2 * HALF), 1)
    mask = (row % FB == column % FB) & (column % HALF < SEGS * FB)

    def rows(b, carry):
        spreaded = dot(spread[...], white[b].reshape(2 * HALF, HALF), NT)
        own[b] = jnp.where(mask, spreaded, 0.0).astype(BF16)
        return carry

    outs = []
    for i in range(CUTS):
        cut = pl.ds(i * (BLOCKS // CUTS), BLOCKS // CUTS)
        lax.fori_loop(i * (BLOCKS // CUTS), (i + 1) * (BLOCKS // CUTS), rows, 0, unroll=8)
        outs.append(pltpu.make_async_copy(own.at[cut], own_hbm.at[cut], own_sem.at[i]))
        outs[-1].start()
    for o in outs:
        o.wait()
    for c in kept:
        c.wait()


def scratch():
    return [
        pltpu.VMEM((8, SHARDS, OWN, SHARD), BF16),
        pltpu.VMEM((2, 4, SECT, 256), BF16),
        pltpu.VMEM((2, 4, SECT, SECT), F32),
        pltpu.VMEM((2, 2, 4, TILES, FB, SECT), F32),
    ]


VMEM_SPEC = pl.BlockSpec(memory_space=pltpu.VMEM)
ANY_SPEC = pl.BlockSpec(memory_space=pl.ANY)
HBM_SPEC = pl.BlockSpec(memory_space=pltpu.HBM)
CUTS = 4
SMEM_SPEC = pl.BlockSpec(memory_space=pltpu.SMEM)


def near_spectra(offsets, blocks, forward):
    spread = (np.arange(HALF)[:, None] // FB == np.arange(HALF)[None, :]).astype(jnp.bfloat16)
    return pl.pallas_call(
        near_kernel,
        out_shape=[
            jax.ShapeDtypeStruct((BLOCKS, 2, PAIRS, 2 * FB, HALF), BF16),
            jax.ShapeDtypeStruct((BLOCKS, HALF, SECT), BF16),
            jax.ShapeDtypeStruct((8, 128), F32),
        ],
        in_specs=[SMEM_SPEC] + [ANY_SPEC] * 8 + [VMEM_SPEC] * 2,
        out_specs=[HBM_SPEC, HBM_SPEC, VMEM_SPEC],
        scratch_shapes=[
            pltpu.VMEM((BLOCKS, 2, PAIRS, 2 * FB, HALF), BF16),
            pltpu.VMEM((BLOCKS, HALF, SECT), BF16),
        ] + scratch() + [
            pltpu.SemaphoreType.DMA((8,)),
            pltpu.SemaphoreType.DMA((PAIRS,)),
            pltpu.SemaphoreType.DMA((CUTS,)),
        ],
        compiler_params=pltpu.CompilerParams(vmem_limit_bytes=58 * 1024 * 1024),
        cost_estimate=pl.CostEstimate(flops=5_000_000_000, bytes_accessed=7_000_000, transcendentals=0),
        name="near_spectra",
    )(offsets, *blocks, forward, jnp.asarray(spread))


GROUP = 4


def second_kernel(places, offsets, *refs):
    n = len(places)
    blocks, refs = refs[:n], refs[n:]
    (_, white_hbm, own_hbm, forward, inverse, picks, out_hbm, series, piece, part, full, white, own,
     grams, chosen, result, sem, near_sem, own_sem, out_sem) = refs
    copies = []
    core = offsets[SEGS]
    for i, (b, (at, part_of)) in enumerate(zip(blocks, places)):
        first, count = ((0, SHARDS), (core * 8, 8), (8 - core * 8, 8))[part_of]
        copies.append(pltpu.make_async_copy(b, series.at[at, pl.ds(first, count)], sem.at[i]))
    for c in copies:
        c.start()
    near = pltpu.make_async_copy(white_hbm, white.at[:, :, :, :, pl.ds(0, HALF)], near_sem)
    near.start()
    mine = pltpu.make_async_copy(own_hbm, own, own_sem)
    mine.start()
    for c in copies:
        c.wait()
    spectra(offsets, series, forward, piece, part, full, white, slice(HALF, SECT))
    near.wait()
    mine.wait()

    def gram(b):
        rows = own[b]
        turned = jnp.concatenate([-rows[:, HALF:], rows[:, :HALF]], axis=1)
        both = jnp.concatenate([rows, turned], axis=0)
        return dot(both, white[b].reshape(2 * HALF, SECT), NN).reshape(2, OWN, FB, SECT)

    def pair_of_blocks(b, carry):
        low, high = gram(2 * b), gram(2 * b + 1)
        for k in range(OWN):
            for ri in range(2):
                grams[k, ri, b] = jnp.concatenate([low[ri, k], high[ri, k]], axis=0).astype(BF16)
        return carry

    lax.fori_loop(0, BLOCKS // 2, pair_of_blocks, 0, unroll=16)
    outs = [
        pltpu.make_async_copy(
            result.at[pl.ds(g * GROUP, GROUP)], out_hbm.at[pl.ds(g * GROUP, GROUP)], out_sem.at[g]
        )
        for g in range(OWN // GROUP)
    ]
    for g in range(OWN // GROUP):
        for k in range(g * GROUP, (g + 1) * GROUP):
            crossed = dot(picks[k], grams[k].reshape(2 * NF, SECT), NT)
            chosen[k % GROUP] = crossed.astype(BF16)
        lags = dot(chosen[...].reshape(GROUP * NPART, 2 * NF), inverse[...], NN) * (1.0 / math.sqrt(NF))
        result[g * GROUP:(g + 1) * GROUP] = lags.reshape(GROUP, NPART, NLAG)
        outs[g].start()
    for o in outs:
        o.wait()


def second_half(offsets, blocks, places, token, white, own, forward, inverse, picks):
    n = len(blocks)
    return pl.pallas_call(
        functools.partial(second_kernel, places),
        out_shape=jax.ShapeDtypeStruct((OWN, NPART, NLAG), F32),
        in_specs=[SMEM_SPEC] + [ANY_SPEC] * (n + 1) + [HBM_SPEC] * 2 + [VMEM_SPEC] * 3,
        out_specs=ANY_SPEC,
        scratch_shapes=scratch() + [
            pltpu.VMEM((BLOCKS, 2, PAIRS, 2 * FB, SECT), BF16),
            pltpu.VMEM((BLOCKS, HALF, SECT), BF16),
            pltpu.VMEM((OWN, 2, BLOCKS // 2, 2 * FB, SECT), BF16),
            pltpu.VMEM((GROUP, NPART, 2 * NF), BF16),
            pltpu.VMEM((OWN, NPART, NLAG), F32),
            pltpu.SemaphoreType.DMA((n,)),
            pltpu.SemaphoreType.DMA,
            pltpu.SemaphoreType.DMA,
            pltpu.SemaphoreType.DMA((OWN // GROUP,)),
        ],
        compiler_params=pltpu.CompilerParams(vmem_limit_bytes=58 * 1024 * 1024),
        cost_estimate=pl.CostEstimate(flops=8_000_000_000, bytes_accessed=20_000_000, transcendentals=0),
        name="far_and_cross",
    )(offsets, *blocks, token, white, own, forward, inverse, picks)


def per_device(record, partners, offsets):
    forward, inverse = (jnp.asarray(t) for t in build_tables())
    place = lax.axis_index("pair")
    core = place % 2
    rows = jnp.transpose(record, (1, 2, 0)).reshape(SHARDS * OWN, SHARD)
    order = np.arange(SHARD) % 128 * 4 + np.arange(SHARD) // 128
    sort = (np.arange(SHARD)[:, None] == order[None, :]).astype(jnp.bfloat16)
    rows = jnp.dot(rows, jnp.asarray(sort), preferred_element_type=BF16)
    mine = lax.all_to_all(
        rows.reshape(SHARDS, OWN, SHARD), "tm", split_axis=0, concat_axis=0, tiled=True
    )

    onward = [(i, (i + 2 - 4 * (i % 2)) % 16) for i in range(16)]
    further = [(i, (i + 4 - 8 * (i % 2)) % 16) for i in range(16)]
    across = [(i, i ^ 1) for i in range(16)]

    def send(v, pairs):
        return lax.ppermute(v, "pair", pairs)

    def half(v):
        return lax.dynamic_slice_in_dim(v, core * 8, 8, 0)

    other = send(mine, across)
    m1, o1 = send(mine, onward), send(other, onward)
    m2, o2 = send(m1, onward), send(o1, onward)
    xm1, xo1 = send(m1, across), send(o1, across)
    m3, o3 = send(m2, onward), send(o2, onward)
    m4, o4 = send(half(m2), further), send(half(o2), further)
    xm2, xo2 = send(m2, across), send(o2, across)
    near = [mine, other, m1, o1, xm1, xo1, m2, o2]
    numbers = jnp.concatenate([offsets, core[None]])
    white, own, token = near_spectra(numbers, near, forward)
    m3, o3, m4, o4, token = lax.optimization_barrier((m3, o3, m4, o4, token))
    xm3, xo3 = send(m3, across), send(o3, across)
    xm4, xo4 = send(m4, across), send(o4, across)
    far = [xm2, xo2, m3, o3, xm3, xo3, m4, xo4, o4, xm4]
    places = [(i, 0) for i in range(6)] + [(6, 1), (6, 2), (7, 1), (7, 2)]

    toward = 2 * (2 * core - 1)
    steps = np.array([0, 0, 1, 1, -1, -1, 2, 2, -2, -2, 3, 3, -3, -3, 4, 4], np.int32)
    swap = np.array([0, 1, 0, 1, 1, 0, 0, 1, 1, 0, 0, 1, 1, 0, 0, 1], np.int32)
    origin = ((place + toward * steps) % 16) ^ swap
    channel = jnp.repeat(origin * OWN, OWN) + np.tile(np.arange(OWN, dtype=np.int32), 16)
    picks = ((partners % SECT)[:, :, None] == channel).astype(BF16)
    return second_half(numbers, far, places, token, white, own, forward, inverse, picks)


def solution(mesh):
    in_specs = (P("tm", None, "pair"), P(("tm", "pair"), None), P())
    out_specs = P(("tm", "pair"), None, None)
    return jax.shard_map(
        per_device, mesh=mesh, in_specs=in_specs, out_specs=out_specs, check_vma=False
    )
```

```python
import functools
import math

import jax
import jax.numpy as jnp
import numpy as np
from jax import lax
from jax.experimental import pallas as pl
from jax.experimental.pallas import tpu as pltpu
from jax.sharding import PartitionSpec as P

SEG = 1024
NF = 512
NLAG = 512
SEGS = 15
PAIRS = 8
NPART = 64
SHARDS = 16
SHARD = 512
SECT = 256
OWN = 16
HALF = 128
FB = 8
BLOCKS = NF // FB
TILES = 16
F32 = jnp.float32
BF16 = jnp.bfloat16
NT = (((1,), (1,)), ((), ()))
NN = (((1,), (0,)), ((), ()))


def slots():
    q = np.arange(128)
    freq = np.concatenate([q, 512 - q, 256 + q, 256 - q])
    freq[128], freq[384] = 128, 384
    sign = np.where(np.arange(512) < 384, 1.0, -1.0)
    return freq, sign


def build_tables():
    samples = np.arange(SEG)
    unit = np.float32(2.0 * math.pi / SEG)
    taper = (0.5 - 0.5 * np.cos(samples.astype(np.float32) * unit)).astype(np.float32)
    q = np.arange(128)
    phase = (q[:, None] * samples[None, :] % SEG).astype(np.float32) * unit
    cosine, sine = taper * np.cos(phase), -taper * np.sin(phase)
    eighth = (128 * samples % SEG).astype(np.float32) * unit
    sine[0] = np.where(samples % 4 == 2, -taper * np.sin(eighth), taper * np.cos(eighth))
    sine[0] = np.where(samples % 4 == 2, -1.0, np.where(samples % 4 == 3, -1.0, 1.0)) * sine[0]
    forward = np.concatenate([cosine, sine]).reshape(256, 256, 4).transpose(2, 0, 1)
    freq, sign = slots()
    lag = np.arange(NLAG) - NLAG // 2
    lag_phase = (freq[:, None] * lag[None, :] % SEG).astype(np.float32) * unit
    inverse = np.concatenate([np.cos(lag_phase), -sign[:, None] * np.sin(lag_phase)])
    return np.ascontiguousarray(forward).astype(jnp.bfloat16), inverse.astype(jnp.bfloat16)


def dot(a, b, dims):
    return lax.dot_general(a, b, dims, preferred_element_type=F32)


def cut_pieces(offsets, series, piece, u, slot):
    lane = lax.broadcasted_iota(jnp.int32, (HALF, 128), 1)
    for s2 in range(2):
        start = offsets[min(2 * u + s2, SEGS - 1)]
        for r in range(4):
            first = start + r
            group = pl.multiple_of((first & 3) * 128, 128)
            at = first >> 2
            tile, off = at >> 7, at & 127
            back = (128 - off) & 127
            keep = lane < 128 - off
            turned = []
            for i in range(3):
                t = jnp.minimum(tile + i, SHARDS - 1)
                rows = series[:, t, :, pl.ds(group, 128)].reshape(HALF, 128)
                turned.append(pltpu.roll(rows.astype(F32), back, 1))
            for i in range(2):
                piece[slot, r, s2 * HALF:(s2 + 1) * HALF, i * 128:(i + 1) * 128] = jnp.where(
                    keep, turned[i], turned[i + 1]
                ).astype(BF16)


def transform(forward, piece, part, slot):
    for r in range(4):
        part[slot, r] = dot(forward[r], piece[slot, r], NT)


def whiten(part, full, white, u, slot, lanes):
    head = lax.broadcasted_iota(jnp.int32, (FB, SECT), 0) == 0
    total = jnp.zeros((FB, SECT), F32)
    for i in range(TILES):
        c = [part[slot, r, i * FB:(i + 1) * FB, :] for r in range(4)]
        s = [part[slot, r, HALF + i * FB:HALF + (i + 1) * FB, :] for r in range(4)]
        a, b = c[0] + c[2], c[0] - c[2]
        e, g = s[0] + s[2], s[0] - s[2]
        d, k = c[1] - c[3], s[1] - s[3]
        p, h = c[1] + c[3], s[1] + s[3]
        re = [a + p, a - p, b + k, b - k]
        im = [e + h, h - e, g - d, g + d]
        if i == 0:
            im[0] = jnp.where(head, 0.0, im[0])
            re[1] = jnp.where(head, s[0] + k, re[1])
            im[1] = jnp.where(head, -h - s[2], im[1])
            re[2] = jnp.where(head, b, re[2])
            im[2] = jnp.where(head, -d, im[2])
            re[3] = jnp.where(head, s[0] - k, re[3])
            im[3] = jnp.where(head, h - s[2], im[3])
        for j in range(4):
            full[0, j, i], full[1, j, i] = re[j], im[j]
            total += re[j] * re[j] + im[j] * im[j]
    water = jnp.sum(total, axis=0, keepdims=True) * (1.0 / NF) + 1e-06
    for i in range(TILES):
        for j in range(4):
            re, im = full[0, j, i], full[1, j, i]
            factor = lax.rsqrt(re * re + im * im + water)
            for ri, v in ((0, re * factor), (1, im * factor)):
                white[j * TILES + i, ri, u, :, lanes] = jnp.concatenate(
                    [v[:, :HALF], v[:, HALF:]], axis=0
                ).astype(BF16)


def spectra(offsets, series, forward, piece, part, full, white, lanes, after=lambda u: None):
    cut_pieces(offsets, series, piece, 0, 0)
    for u in range(PAIRS):
        transform(forward, piece, part, u % 2)
        if u + 1 < PAIRS:
            cut_pieces(offsets, series, piece, u + 1, (u + 1) % 2)
        whiten(part, full.at[u % 2], white, u, u % 2, lanes)
        after(u)


def near_kernel(offsets, *refs):
    blocks, refs = refs[:8], refs[8:]
    forward, _, white_hbm, token, white, series, piece, part, full, sem, near_sem = refs
    copies = [pltpu.make_async_copy(b, series.at[i], sem.at[i]) for i, b in enumerate(blocks)]
    for c in copies:
        c.start()
    for c in copies:
        c.wait()
    kept = [
        pltpu.make_async_copy(white.at[:, :, u], white_hbm.at[:, :, u], near_sem.at[u])
        for u in range(PAIRS)
    ]
    spectra(
        offsets, series, forward, piece, part, full, white, slice(0, HALF), lambda u: kept[u].start()
    )
    token[...] = jnp.zeros((8, 128), F32)
    for c in kept:
        c.wait()


def scratch():
    return [
        pltpu.VMEM((8, SHARDS, OWN, SHARD), BF16),
        pltpu.VMEM((2, 4, SECT, 256), BF16),
        pltpu.VMEM((2, 4, SECT, SECT), F32),
        pltpu.VMEM((2, 2, 4, TILES, FB, SECT), F32),
    ]


VMEM_SPEC = pl.BlockSpec(memory_space=pltpu.VMEM)
ANY_SPEC = pl.BlockSpec(memory_space=pl.ANY)
HBM_SPEC = pl.BlockSpec(memory_space=pltpu.HBM)
SMEM_SPEC = pl.BlockSpec(memory_space=pltpu.SMEM)


def near_spectra(offsets, blocks, forward, picks):
    return pl.pallas_call(
        near_kernel,
        out_shape=[
            jax.ShapeDtypeStruct((BLOCKS, 2, PAIRS, 2 * FB, HALF), BF16),
            jax.ShapeDtypeStruct((8, 128), F32),
        ],
        in_specs=[SMEM_SPEC] + [ANY_SPEC] * 8 + [VMEM_SPEC, ANY_SPEC],
        out_specs=[HBM_SPEC, VMEM_SPEC],
        scratch_shapes=[
            pltpu.VMEM((BLOCKS, 2, PAIRS, 2 * FB, HALF), BF16),
        ] + scratch() + [
            pltpu.SemaphoreType.DMA((8,)),
            pltpu.SemaphoreType.DMA((PAIRS,)),
        ],
        compiler_params=pltpu.CompilerParams(vmem_limit_bytes=58 * 1024 * 1024),
        cost_estimate=pl.CostEstimate(flops=5_000_000_000, bytes_accessed=7_000_000, transcendentals=0),
        name="near_spectra",
    )(offsets, *blocks, forward, picks)


GROUP = 4


def second_kernel(places, offsets, *refs):
    n = len(places)
    blocks, refs = refs[:n], refs[n:]
    (_, white_hbm, forward, spread, inverse, picks, out_hbm, series, piece, part, full, white, own,
     grams, chosen, result, sem, near_sem, out_sem) = refs
    copies = []
    core = offsets[SEGS]
    for i, (b, (at, part_of)) in enumerate(zip(blocks, places)):
        first, count = ((0, SHARDS), (core * 8, 8), (8 - core * 8, 8))[part_of]
        copies.append(pltpu.make_async_copy(b, series.at[at, pl.ds(first, count)], sem.at[i]))
    for c in copies:
        c.start()
    near = pltpu.make_async_copy(white_hbm, white.at[:, :, :, :, pl.ds(0, HALF)], near_sem)
    near.start()
    for c in copies:
        c.wait()
    spectra(offsets, series, forward, piece, part, full, white, slice(HALF, SECT))
    near.wait()
    row = lax.broadcasted_iota(jnp.int32, (HALF, 2 * HALF), 0)
    column = lax.broadcasted_iota(jnp.int32, (HALF, 2 * HALF), 1)
    mask = (row % FB == column % FB) & (column % HALF < SEGS * FB)

    def own_rows(b, carry):
        rows = white[b, :, :, :, :HALF].reshape(2 * HALF, HALF)
        own[b] = jnp.where(mask, dot(spread[...], rows, NT), 0.0).astype(BF16)
        return carry

    lax.fori_loop(0, BLOCKS, own_rows, 0, unroll=8)

    def gram(b):
        rows = own[b]
        turned = jnp.concatenate([-rows[:, HALF:], rows[:, :HALF]], axis=1)
        both = jnp.concatenate([rows, turned], axis=0)
        return dot(both, white[b].reshape(2 * HALF, SECT), NN).reshape(2, OWN, FB, SECT)

    def pair_of_blocks(b, carry):
        low, high = gram(2 * b), gram(2 * b + 1)
        for k in range(OWN):
            for ri in range(2):
                grams[k, ri, b] = jnp.concatenate([low[ri, k], high[ri, k]], axis=0).astype(BF16)
        return carry

    lax.fori_loop(0, BLOCKS // 2, pair_of_blocks, 0, unroll=16)
    outs = [
        pltpu.make_async_copy(
            result.at[pl.ds(g * GROUP, GROUP)], out_hbm.at[pl.ds(g * GROUP, GROUP)], out_sem.at[g]
        )
        for g in range(OWN // GROUP)
    ]
    for g in range(OWN // GROUP):
        for k in range(g * GROUP, (g + 1) * GROUP):
            crossed = dot(picks[k], grams[k].reshape(2 * NF, SECT), NT)
            chosen[k % GROUP] = crossed.astype(BF16)
        lags = dot(chosen[...].reshape(GROUP * NPART, 2 * NF), inverse[...], NN) * (1.0 / math.sqrt(NF))
        result[g * GROUP:(g + 1) * GROUP] = lags.reshape(GROUP, NPART, NLAG)
        outs[g].start()
    for o in outs:
        o.wait()


def second_half(offsets, blocks, places, token, white, forward, inverse, picks):
    spread = (np.arange(HALF)[:, None] // FB == np.arange(HALF)[None, :]).astype(jnp.bfloat16)
    n = len(blocks)
    return pl.pallas_call(
        functools.partial(second_kernel, places),
        out_shape=jax.ShapeDtypeStruct((OWN, NPART, NLAG), F32),
        in_specs=[SMEM_SPEC] + [ANY_SPEC] * (n + 1) + [HBM_SPEC] + [VMEM_SPEC] * 4,
        out_specs=ANY_SPEC,
        scratch_shapes=scratch() + [
            pltpu.VMEM((BLOCKS, 2, PAIRS, 2 * FB, SECT), BF16),
            pltpu.VMEM((BLOCKS, HALF, SECT), BF16),
            pltpu.VMEM((OWN, 2, BLOCKS // 2, 2 * FB, SECT), BF16),
            pltpu.VMEM((GROUP, NPART, 2 * NF), BF16),
            pltpu.VMEM((OWN, NPART, NLAG), F32),
            pltpu.SemaphoreType.DMA((n,)),
            pltpu.SemaphoreType.DMA,
            pltpu.SemaphoreType.DMA((OWN // GROUP,)),
        ],
        compiler_params=pltpu.CompilerParams(vmem_limit_bytes=58 * 1024 * 1024),
        cost_estimate=pl.CostEstimate(flops=8_000_000_000, bytes_accessed=20_000_000, transcendentals=0),
        name="far_and_cross",
    )(offsets, *blocks, token, white, forward, jnp.asarray(spread), inverse, picks)


def per_device(record, partners, offsets):
    forward, inverse = (jnp.asarray(t) for t in build_tables())
    place = lax.axis_index("pair")
    core = place % 2
    rows = jnp.transpose(record, (1, 2, 0)).reshape(SHARDS * OWN, SHARD)
    order = np.arange(SHARD) % 128 * 4 + np.arange(SHARD) // 128
    sort = (np.arange(SHARD)[:, None] == order[None, :]).astype(jnp.bfloat16)
    rows = jnp.dot(rows, jnp.asarray(sort), preferred_element_type=BF16)
    mine = lax.all_to_all(
        rows.reshape(SHARDS, OWN, SHARD), "tm", split_axis=0, concat_axis=0, tiled=True
    )

    onward = [(i, (i + 2 - 4 * (i % 2)) % 16) for i in range(16)]
    further = [(i, (i + 4 - 8 * (i % 2)) % 16) for i in range(16)]
    across = [(i, i ^ 1) for i in range(16)]

    def send(v, pairs):
        return lax.ppermute(v, "pair", pairs)

    def half(v):
        return lax.dynamic_slice_in_dim(v, core * 8, 8, 0)

    other = send(mine, across)
    m1, o1 = send(mine, onward), send(other, onward)
    m2, o2 = send(m1, onward), send(o1, onward)
    xm1, xo1 = send(m1, across), send(o1, across)
    m3, o3 = send(m2, onward), send(o2, onward)
    m4, o4 = send(half(m2), further), send(half(o2), further)
    xm2, xo2 = send(m2, across), send(o2, across)
    near = [mine, other, m1, o1, xm1, xo1, m2, o2]
    numbers = jnp.concatenate([offsets, core[None]])
    toward = 2 * (2 * core - 1)
    steps = np.array([0, 0, 1, 1, -1, -1, 2, 2, -2, -2, 3, 3, -3, -3, 4, 4], np.int32)
    swap = np.array([0, 1, 0, 1, 1, 0, 0, 1, 1, 0, 0, 1, 1, 0, 0, 1], np.int32)
    origin = ((place + toward * steps) % 16) ^ swap
    channel = jnp.repeat(origin * OWN, OWN) + np.tile(np.arange(OWN, dtype=np.int32), 16)
    picks = ((partners % SECT)[:, :, None] == channel).astype(BF16)
    white, token = near_spectra(numbers, near, forward, picks)
    m3, o3, m4, o4, token = lax.optimization_barrier((m3, o3, m4, o4, token))
    xm3, xo3 = send(m3, across), send(o3, across)
    xm4, xo4 = send(m4, across), send(o4, across)
    far = [xm2, xo2, m3, o3, xm3, xo3, m4, xo4, o4, xm4]
    places = [(i, 0) for i in range(6)] + [(6, 1), (6, 2), (7, 1), (7, 2)]

    return second_half(numbers, far, places, token, white, forward, inverse, picks)


def solution(mesh):
    in_specs = (P("tm", None, "pair"), P(("tm", "pair"), None), P())
    out_specs = P(("tm", "pair"), None, None)
    return jax.shard_map(
        per_device, mesh=mesh, in_specs=in_specs, out_specs=out_specs, check_vma=False
    )
```
